128 devices in a mesh: row: 16 (over x_hi, y, core), col: 8 (over x_lo, z).
Axes of the slice: x: 4 (x_hi: 2, x_lo: 2; x = x_hi * 2 + x_lo), y: 4, z: 4, core: 2. Of those that a mesh axis runs over, the one named last changes fastest.
Arguments:
- gate_pre: bfloat16 [2048, 26624], P('row', 'col'), may hold values from -6 to 6
- up_pre: bfloat16 [2048, 26624], P('row', 'col'), may hold values from -6 to 6
- grad_out: bfloat16 [2048, 16384], P('row', 'col'), may hold values from -6 to 6
- down_weight: bfloat16 [16384, 26624], P('row', 'col'), may hold values from -0.046875 to 0.046875
Outputs:
- grad_gate: bfloat16 [2048, 26624], P('row', 'col')
- grad_up: bfloat16 [2048, 26624], P('row', 'col')
- grad_down: bfloat16 [16384, 26624], P('row', 'col')
The draws below stay inside these ranges and needn't reach their ends.
All inputs are finite; a program needn't handle non-finite values.
Results may differ from the reference program's by a relative error of at most 0.023.
Values may be sent and summed in bfloat16 or wider, within the bound.
No kernel may reach another device: no remote copies, remote signals or barrier semaphores. Data moves between devices by JAX's collectives and lax.ppermute only.
A program may use at most 320 MiB of HBM per device.

```python
import math
import jax
import jax.numpy as jnp
from jax import lax

D = 16384
FF = 26624
TOKENS = 2048
N_ROW = 16


def level_of(rng, shape, pieces, low, high):
    factor_of, own = 1.0, jax.random.fold_in(rng, 6)
    for axis_at, blocks in pieces:
        draws = jnp.exp(jax.random.uniform(jax.random.fold_in(own, axis_at), (blocks,), jnp.float32, low / len(pieces), high / len(pieces)))
        factor_of = factor_of * jnp.repeat(draws, shape[axis_at] // blocks).reshape([-1 if axis == axis_at else 1 for axis in range(len(shape))])
    return factor_of


def bell_draw(key, dims, deviation, reach, pieces=(), kind=jnp.bfloat16):
    loudness = level_of(key, dims, pieces, -0.22, 0.18) if pieces else 1.0
    values = jax.random.normal(key, dims, jnp.float32) * deviation * loudness
    return jnp.minimum(jnp.maximum(values, -reach), reach).astype(kind)


def setup_inputs(seed: int = 0) -> dict:
    key_of = jax.random.split(jax.random.key(seed), 5)
    gate_pre = bell_draw(key_of[0], (TOKENS, FF), 1.0, 6.0, ((0, 16), (1, 8)))
    up_pre = bell_draw(key_of[1], (TOKENS, FF), 1.0, 6.0, ((0, 16), (1, 8)))
    grad_out = bell_draw(key_of[2], (TOKENS, D), 1.0, 6.0, ((0, 16), (1, 8)))
    down_weight = bell_draw(key_of[3], (D, FF), D ** -0.5, 0.046875, ((0, 16), (1, 8)))
    return dict(gate_pre=gate_pre, up_pre=up_pre, grad_out=grad_out, down_weight=down_weight)


def reference(gate_pre, up_pre, grad_out, down_weight):
    gate_value = gate_pre.astype(jnp.float32)
    up_value = up_pre.astype(jnp.float32)
    gate_sig = jax.nn.sigmoid(gate_value)
    activated = gate_value * gate_sig
    hidden = (activated * up_value).astype(jnp.bfloat16)
    block_width = grad_out.shape[1] // N_ROW

    def add_block(running, block_index):
        offset = (block_index * block_width).astype(jnp.int32)
        left_rows = lax.dynamic_slice_in_dim(grad_out, offset, block_width, 1)
        right_rows = lax.dynamic_slice_in_dim(down_weight, offset, block_width, 0)
        summand = jnp.dot(left_rows, right_rows, preferred_element_type=jnp.float32).astype(jnp.bfloat16)
        summand = lax.optimization_barrier(summand)
        return (running + summand.astype(jnp.float32), None)
    initial = jnp.zeros((grad_out.shape[0], down_weight.shape[1]), jnp.float32)
    grad_hidden, _ = lax.scan(add_block, initial, jnp.arange(N_ROW, dtype=jnp.int32))
    grad_gate = (grad_hidden * up_value * gate_sig * (1.0 + gate_value * (1.0 - gate_sig))).astype(jnp.bfloat16)
    grad_up = (grad_hidden * activated).astype(jnp.bfloat16)
    scaling = 1.0 / math.sqrt(grad_out.shape[0])
    grad_down = (jnp.dot(grad_out.T, hidden, preferred_element_type=jnp.float32) * scaling).astype(jnp.bfloat16)
    return (grad_gate, grad_up, grad_down)
```

```python
import math

import jax
import jax.numpy as jnp
from jax import lax
from jax.sharding import PartitionSpec as P

NX, NY, NC, NL, NZ = 2, 4, 2, 2, 4
AXES = ("row", "col")
F32, BF16 = jnp.float32, jnp.bfloat16


def linear(xh, y, core, xl, z):
    return (((xh * NY + y) * NC + core) * NL + xl) * NZ + z


def send(value, target):
    pairs = []
    for xh in range(NX):
        for y in range(NY):
            for core in range(NC):
                for xl in range(NL):
                    for z in range(NZ):
                        to = target(xh, y, core, xl, z)
                        pairs.append((linear(xh, y, core, xl, z), linear(*to)))
    return lax.ppermute(value, AXES, pairs)


def swap_core(value):
    return send(value, lambda xh, y, core, xl, z: (xh, y, 1 - core, xl, z))


def swap_xh(value):
    return send(value, lambda xh, y, core, xl, z: (1 - xh, y, core, xl, z))


def swap_xl(value):
    return send(value, lambda xh, y, core, xl, z: (xh, y, core, 1 - xl, z))


def shift_y(value, d):
    return send(value, lambda xh, y, core, xl, z: (xh, (y + d) % NY, core, xl, z))


def shift_z(value, d):
    return send(value, lambda xh, y, core, xl, z: (xh, y, core, xl, (z + d) % NZ))


def transpose_chips(value):
    return send(value, lambda xh, y, core, xl, z: (xl, z, core, xh, y))


def pick(array, index):
    return lax.dynamic_index_in_dim(array, index, 0, keepdims=False)


def put(array, chunk, *index):
    start = (*index, *([0] * (array.ndim - len(index))))
    return lax.dynamic_update_slice(array, chunk.reshape((1,) * len(index) + chunk.shape), start)


def on_device(gate_pre, up_pre, grad_out, down_weight):
    row, col = lax.axis_index("row"), lax.axis_index("col")
    xh, y, core = row // (NY * NC), (row // NC) % NY, row % NC
    xl, z = col // NZ, col % NZ
    first_core = core == 0
    tokens, width = grad_out.shape
    depth, units = down_weight.shape
    half = units // 2

    own = transpose_chips(grad_out)
    far = swap_xl(own)
    blocks = jnp.zeros((NX, NY, NC, tokens, width), BF16)
    for group, (base, side) in enumerate(((own, xl), (far, 1 - xl))):
        arrived = [base] + [shift_z(base, d) for d in (1, 3, 2)]
        other = swap_core(jnp.stack(arrived))
        for at, d in enumerate((0, 1, 3, 2)):
            place = (z - d) % NZ
            blocks = put(blocks, arrived[at], side, place, core)
            blocks = put(blocks, other[at], side, place, 1 - core)

    keep = jnp.where(first_core, down_weight[:, :half], down_weight[:, half:])
    give = jnp.where(first_core, down_weight[:, half:], down_weight[:, :half])
    got = swap_core(give)
    weight = jnp.where(
        first_core, jnp.concatenate([keep, got], 0), jnp.concatenate([got, keep], 0)
    )

    gate_value = gate_pre.astype(F32)
    up_value = up_pre.astype(F32)
    gate_sig = jax.nn.sigmoid(gate_value)
    activated = gate_value * gate_sig
    hidden = (activated * up_value).astype(BF16)
    hidden_all = lax.all_gather(hidden, "row", axis=0, tiled=True)

    def partial(side):
        rows = pick(blocks, side).reshape(NY * NC * tokens, width)
        out = jnp.dot(rows, weight, preferred_element_type=F32).astype(BF16)
        return out.reshape(NY, NC * tokens, half)

    cut = NC * tokens * 5 // 8
    there, here = partial(1 - xh), partial(xh)
    x_got = swap_xh(there[:, :cut])
    y_got = {}
    for d in (1, 3, 2):
        to = (y + d) % NY
        y_got[d] = shift_y(jnp.stack([pick(there, to)[cut:], pick(here, to)[cut:]]), d)
    y_last = {}
    for d in (1, 3, 2):
        to = (y + d) % NY
        joined = pick(here, to)[:cut].astype(F32) + pick(x_got, to).astype(F32)
        y_last[d] = shift_y(joined.astype(BF16), d)
    across = pick(there, y)[cut:].astype(F32) + sum(y_got[d][0].astype(F32) for d in (1, 3, 2))
    x_last = swap_xh(across.astype(BF16))
    top = (
        pick(here, y)[:cut].astype(F32)
        + pick(x_got, y).astype(F32)
        + sum(y_last[d].astype(F32) for d in (1, 3, 2))
    )
    bottom = (
        pick(here, y)[cut:].astype(F32)
        + sum(y_got[d][1].astype(F32) for d in (1, 3, 2))
        + x_last.astype(F32)
    )
    summed = jnp.concatenate([top, bottom], 0).astype(BF16)
    mine = jnp.where(first_core, summed[:tokens], summed[tokens:])
    other = swap_core(jnp.where(first_core, summed[tokens:], summed[:tokens]))
    grad_hidden = jnp.where(
        first_core, jnp.concatenate([mine, other], 1), jnp.concatenate([other, mine], 1)
    ).astype(F32)
    grad_gate = (grad_hidden * up_value * gate_sig * (1.0 + gate_value * (1.0 - gate_sig))).astype(
        BF16
    )
    grad_up = (grad_hidden * activated).astype(BF16)

    flat = blocks.reshape(NX * NY * NC * tokens, width)
    features = jnp.where(first_core, flat[:, :depth], flat[:, depth:])
    product = lax.dot_general(
        features, hidden_all, (((0,), (0,)), ((), ())), preferred_element_type=F32
    )
    grad_down = (product * (1.0 / math.sqrt(flat.shape[0]))).astype(BF16)
    return (grad_gate, grad_up, grad_down)


def solution(mesh):
    in_specs = (P("row", "col"), P("row", "col"), P("row", "col"), P("row", "col"))
    out_specs = (P("row", "col"), P("row", "col"), P("row", "col"))
    return jax.shard_map(
        on_device, mesh=mesh, in_specs=in_specs, out_specs=out_specs, check_vma=False
    )
```

```python
import math

import jax
import jax.numpy as jnp
from jax import lax
from jax.sharding import PartitionSpec as P

NX, NY, NC, NL, NZ = 2, 4, 2, 2, 4
AXES = ("row", "col")
F32, BF16 = jnp.float32, jnp.bfloat16


def linear(xh, y, core, xl, z):
    return (((xh * NY + y) * NC + core) * NL + xl) * NZ + z


def send(value, target):
    pairs = []
    for xh in range(NX):
        for y in range(NY):
            for core in range(NC):
                for xl in range(NL):
                    for z in range(NZ):
                        to = target(xh, y, core, xl, z)
                        pairs.append((linear(xh, y, core, xl, z), linear(*to)))
    return lax.ppermute(value, AXES, pairs)


def swap_core(value):
    return send(value, lambda xh, y, core, xl, z: (xh, y, 1 - core, xl, z))


def swap_xh(value):
    return send(value, lambda xh, y, core, xl, z: (1 - xh, y, core, xl, z))


def swap_xl(value):
    return send(value, lambda xh, y, core, xl, z: (xh, y, core, 1 - xl, z))


def shift_y(value, d):
    return send(value, lambda xh, y, core, xl, z: (xh, (y + d) % NY, core, xl, z))


def shift_z(value, d):
    return send(value, lambda xh, y, core, xl, z: (xh, y, core, xl, (z + d) % NZ))


def transpose_chips(value):
    return send(value, lambda xh, y, core, xl, z: (xl, z, core, xh, y))


def pick(array, index):
    return lax.dynamic_index_in_dim(array, index, 0, keepdims=False)


def put(array, chunk, *index):
    start = (*index, *([0] * (array.ndim - len(index))))
    return lax.dynamic_update_slice(array, chunk.reshape((1,) * len(index) + chunk.shape), start)


def swish(gate_value):
    gate_sig = jax.nn.sigmoid(gate_value)
    return gate_value * gate_sig, gate_sig


def on_device(gate_pre, up_pre, grad_out, down_weight):
    row, col = lax.axis_index("row"), lax.axis_index("col")
    xh, y, core = row // (NY * NC), (row // NC) % NY, row % NC
    xl, z = col // NZ, col % NZ
    first_core = core == 0
    tokens, width = grad_out.shape
    depth, units = down_weight.shape
    half = units // 2

    hidden = (swish(gate_pre.astype(F32))[0] * up_pre.astype(F32)).astype(BF16)
    hidden, grad_out = lax.optimization_barrier((hidden, grad_out))
    hidden_all = lax.all_gather(hidden, "row", axis=0, tiled=True)

    own = transpose_chips(grad_out)
    near = [own] + [shift_z(own, d) for d in (1, 3, 2)]
    near.append(swap_xl(own))
    near = lax.optimization_barrier(near)
    far = [near.pop()]
    near_other = swap_core(jnp.stack(near))
    far += [shift_z(far[0], d) for d in (1, 3, 2)]
    far, near_other = lax.optimization_barrier((far, near_other))
    far_other = swap_core(jnp.stack(far))
    blocks = jnp.zeros((NX, NY, NC, tokens, width), BF16)
    for arrived, other, side in ((near, near_other, xl), (far, far_other, 1 - xl)):
        for at, d in enumerate((0, 1, 3, 2)):
            place = (z - d) % NZ
            blocks = put(blocks, arrived[at], side, place, core)
            blocks = put(blocks, other[at], side, place, 1 - core)

    keep = jnp.where(first_core, down_weight[:, :half], down_weight[:, half:])
    give = jnp.where(first_core, down_weight[:, half:], down_weight[:, :half])
    got = swap_core(give)
    weight = jnp.where(
        first_core, jnp.concatenate([keep, got], 0), jnp.concatenate([got, keep], 0)
    )

    def partial(side):
        rows = pick(blocks, side).reshape(NY * NC * tokens, width)
        out = jnp.dot(rows, weight, preferred_element_type=F32).astype(BF16)
        return out.reshape(NY, NC * tokens, half)

    cut = NC * tokens // 2
    there, here = partial(1 - xh), partial(xh)
    x_got = swap_xh(there[:, :cut])
    y_got = {}
    for d in (1, 3, 2):
        to = (y + d) % NY
        y_got[d] = shift_y(jnp.stack([pick(there, to)[cut:], pick(here, to)[cut:]]), d)
    y_last = {}
    for d in (1, 3, 2):
        to = (y + d) % NY
        joined = pick(here, to)[:cut].astype(F32) + pick(x_got, to).astype(F32)
        y_last[d] = shift_y(joined.astype(BF16), d)
    across = pick(there, y)[cut:].astype(F32) + sum(y_got[d][0].astype(F32) for d in (1, 3, 2))
    x_last = swap_xh(across.astype(BF16))
    top = (
        pick(here, y)[:cut].astype(F32)
        + pick(x_got, y).astype(F32)
        + sum(y_last[d].astype(F32) for d in (1, 3, 2))
    )
    bottom = (
        pick(here, y)[cut:].astype(F32)
        + sum(y_got[d][1].astype(F32) for d in (1, 3, 2))
        + x_last.astype(F32)
    )
    summed = jnp.concatenate([top, bottom], 0).astype(BF16)
    mine = jnp.where(first_core, summed[:tokens], summed[tokens:])
    other = swap_core(jnp.where(first_core, summed[tokens:], summed[:tokens]))
    grad_hidden = jnp.where(
        first_core, jnp.concatenate([mine, other], 1), jnp.concatenate([other, mine], 1)
    ).astype(F32)
    gate_pre, up_pre, grad_hidden = lax.optimization_barrier((gate_pre, up_pre, grad_hidden))
    gate_value, up_value = gate_pre.astype(F32), up_pre.astype(F32)
    activated, gate_sig = swish(gate_value)
    grad_gate = (grad_hidden * up_value * gate_sig * (1.0 + gate_value * (1.0 - gate_sig))).astype(
        BF16
    )
    grad_up = (grad_hidden * activated).astype(BF16)

    flat = blocks.reshape(NX * NY * NC * tokens, width)
    features = jnp.where(first_core, flat[:, :depth], flat[:, depth:])
    product = lax.dot_general(
        features, hidden_all, (((0,), (0,)), ((), ())), preferred_element_type=F32
    )
    grad_down = (product * (1.0 / math.sqrt(flat.shape[0]))).astype(BF16)
    return (grad_gate, grad_up, grad_down)


def solution(mesh):
    in_specs = (P("row", "col"), P("row", "col"), P("row", "col"), P("row", "col"))
    out_specs = (P("row", "col"), P("row", "col"), P("row", "col"))
    return jax.shard_map(
        on_device, mesh=mesh, in_specs=in_specs, out_specs=out_specs, check_vma=False
    )
```

```python
import math

import jax
import jax.numpy as jnp
from jax import lax
from jax.sharding import PartitionSpec as P

NX, NY, NC, NL, NZ = 2, 4, 2, 2, 4
AXES = ("row", "col")
F32, BF16 = jnp.float32, jnp.bfloat16


def linear(xh, y, core, xl, z):
    return (((xh * NY + y) * NC + core) * NL + xl) * NZ + z


def send(value, target):
    pairs = []
    for xh in range(NX):
        for y in range(NY):
            for core in range(NC):
                for xl in range(NL):
                    for z in range(NZ):
                        to = target(xh, y, core, xl, z)
                        pairs.append((linear(xh, y, core, xl, z), linear(*to)))
    return lax.ppermute(value, AXES, pairs)


def swap_core(value):
    return send(value, lambda xh, y, core, xl, z: (xh, y, 1 - core, xl, z))


def swap_xh(value):
    return send(value, lambda xh, y, core, xl, z: (1 - xh, y, core, xl, z))


def swap_xl(value):
    return send(value, lambda xh, y, core, xl, z: (xh, y, core, 1 - xl, z))


def shift_y(value, d):
    return send(value, lambda xh, y, core, xl, z: (xh, (y + d) % NY, core, xl, z))


def shift_z(value, d):
    return send(value, lambda xh, y, core, xl, z: (xh, y, core, xl, (z + d) % NZ))


def transpose_chips(value):
    return send(value, lambda xh, y, core, xl, z: (xl, z, core, xh, y))


def pick(array, index):
    return lax.dynamic_index_in_dim(array, index, 0, keepdims=False)


def put(array, chunk, *index):
    start = (*index, *([0] * (array.ndim - len(index))))
    return lax.dynamic_update_slice(array, chunk.reshape((1,) * len(index) + chunk.shape), start)


def swish(gate_value):
    gate_sig = jax.nn.sigmoid(gate_value)
    return gate_value * gate_sig, gate_sig


def on_device(gate_pre, up_pre, grad_out, down_weight):
    row, col = lax.axis_index("row"), lax.axis_index("col")
    xh, y, core = row // (NY * NC), (row // NC) % NY, row % NC
    xl, z = col // NZ, col % NZ
    first_core = core == 0
    tokens, width = grad_out.shape
    depth, units = down_weight.shape
    half = units // 2

    moves = (1, 3, 2)

    hidden = (swish(gate_pre.astype(F32))[0] * up_pre.astype(F32)).astype(BF16)
    grad_out, hidden = lax.optimization_barrier((grad_out, hidden))
    own = transpose_chips(grad_out)
    hidden_all = lax.all_gather(hidden, "row", axis=0, tiled=True)

    keep = jnp.where(first_core, down_weight[:, :half], down_weight[:, half:])
    give = jnp.where(first_core, down_weight[:, half:], down_weight[:, :half])
    own, give = lax.optimization_barrier((own, give))
    got = swap_core(give)
    weight = jnp.where(
        first_core, jnp.concatenate([keep, got], 0), jnp.concatenate([got, keep], 0)
    )

    near = {0: own, **{d: shift_z(own, d) for d in moves}}
    far = {0: swap_xl(own)}
    near[1], far[0], weight = lax.optimization_barrier((near[1], far[0], weight))
    far.update({d: shift_z(far[0], d) for d in moves})

    def partial(rows):
        out = jnp.dot(rows.reshape(-1, width), weight, preferred_element_type=F32)
        return out.astype(BF16).reshape(*rows.shape[:-1], half)

    near_here = xl == xh
    at = [(z - y - d) % NZ for d in range(NY)]

    near_mine = jnp.stack([near[d] for d in range(NZ)])
    near_other = swap_core(near_mine)
    near_up, near_down = partial(near_mine), partial(near_other)
    near_got = {d: shift_y(pick(near_down, at[d]), d) for d in (1, 3)}
    far, near_up, near_down = lax.optimization_barrier((far, near_up, near_down))
    far_mine = jnp.stack([far[d] for d in range(NZ)])
    far_other = swap_core(far_mine)
    far_up, far_down = partial(far_mine), partial(far_other)
    there_up = jnp.where(near_here, far_up, near_up)
    x_got = swap_xh(there_up)
    near_got[2] = shift_y(pick(near_down, at[2]), 2)
    far_got = {d: shift_y(pick(far_down, at[d]), d) for d in moves}
    stacks, _, _ = lax.optimization_barrier(
        ((near_mine, near_other, far_mine, far_other), there_up, far_down)
    )
    here_up = jnp.where(near_here, near_up, far_up)

    features = jnp.zeros((NX, NY, NC, tokens, depth), BF16)
    for i, stack in enumerate(stacks):
        side = xl if i < 2 else 1 - xl
        owner = core if i % 2 == 0 else 1 - core
        block = jnp.where(first_core, stack[..., :depth], stack[..., depth:])
        for d in range(NZ):
            features = put(features, block[d], side, (z - d) % NZ, owner)
    features = features.reshape(NX * NY * NC * tokens, depth)
    product = lax.dot_general(
        features, hidden_all, (((0,), (0,)), ((), ())), preferred_element_type=F32
    )
    grad_down = (product * (1.0 / math.sqrt(features.shape[0]))).astype(BF16)
    x_got, near_got, far_got, here_up, grad_down = lax.optimization_barrier(
        (x_got, near_got, far_got, here_up, grad_down)
    )

    def joined(d):
        return pick(here_up, at[d]).astype(F32) + pick(x_got, at[d]).astype(F32)

    last_send = {d: joined(d).astype(BF16) for d in moves}
    y_last = {d: shift_y(last_send[d], d) for d in moves}
    near_sum, far_sum = (
        pick(block, at[0]).astype(F32) + sum(got[d].astype(F32) for d in moves)
        for block, got in ((near_down, near_got), (far_down, far_got))
    )
    across = jnp.where(near_here, far_sum, near_sum).astype(BF16)
    x_last = swap_xh(across)
    rest = jnp.where(near_here, near_sum, far_sum) + x_last.astype(F32)
    other = swap_core(rest.astype(BF16))

    y_last, other, grad_down = lax.optimization_barrier((y_last, other, grad_down))

    mine = joined(0) + sum(y_last[d].astype(F32) for d in moves)
    other = other.astype(F32)
    grad_hidden = jnp.where(
        first_core, jnp.concatenate([mine, other], 1), jnp.concatenate([other, mine], 1)
    )
    gate_pre, up_pre, grad_hidden = lax.optimization_barrier((gate_pre, up_pre, grad_hidden))
    gate_value, up_value = gate_pre.astype(F32), up_pre.astype(F32)
    activated, gate_sig = swish(gate_value)
    grad_gate = (grad_hidden * up_value * gate_sig * (1.0 + gate_value * (1.0 - gate_sig))).astype(
        BF16
    )
    grad_up = (grad_hidden * activated).astype(BF16)

    return (grad_gate, grad_up, grad_down)


def solution(mesh):
    in_specs = (P("row", "col"), P("row", "col"), P("row", "col"), P("row", "col"))
    out_specs = (P("row", "col"), P("row", "col"), P("row", "col"))
    return jax.shard_map(
        on_device, mesh=mesh, in_specs=in_specs, out_specs=out_specs, check_vma=False
    )
```

```python
import functools
import math

import jax
import jax.numpy as jnp
from jax import lax
from jax.experimental import pallas as pl
from jax.experimental.pallas import tpu as pltpu
from jax.sharding import PartitionSpec as P

NX, NY, NC, NL, NZ = 2, 4, 2, 2, 4
AXES = ("row", "col")
PART = 0.5
F32, BF16 = jnp.float32, jnp.bfloat16


def linear(xh, y, core, xl, z):
    return (((xh * NY + y) * NC + core) * NL + xl) * NZ + z


def send(value, target):
    pairs = []
    for xh in range(NX):
        for y in range(NY):
            for core in range(NC):
                for xl in range(NL):
                    for z in range(NZ):
                        to = target(xh, y, core, xl, z)
                        pairs.append((linear(xh, y, core, xl, z), linear(*to)))
    return lax.ppermute(value, AXES, pairs)


def swap_core(value):
    return send(value, lambda xh, y, core, xl, z: (xh, y, 1 - core, xl, z))


def swap_xh(value):
    return send(value, lambda xh, y, core, xl, z: (1 - xh, y, core, xl, z))


def swap_xh_core(value):
    return send(value, lambda xh, y, core, xl, z: (1 - xh, y, 1 - core, xl, z))


def swap_xl(value):
    return send(value, lambda xh, y, core, xl, z: (xh, y, core, 1 - xl, z))


def shift_y(value, d):
    return send(value, lambda xh, y, core, xl, z: (xh, (y + d) % NY, core, xl, z))


def shift_z(value, d):
    return send(value, lambda xh, y, core, xl, z: (xh, y, core, xl, (z + d) % NZ))


def transpose_chips(value):
    return send(value, lambda xh, y, core, xl, z: (xl, z, core, xh, y))


def pick(array, index):
    return lax.dynamic_index_in_dim(array, index, 0, keepdims=False)


def put(array, chunk, *index):
    start = (*index, *([0] * (array.ndim - len(index))))
    return lax.dynamic_update_slice(array, chunk.reshape((1,) * len(index) + chunk.shape), start)


def block_of(group, last, e):
    return jnp.where(e == 2, last, pick(group, jnp.minimum(e, 2)))


def swish(gate_value):
    gate_sig = jax.nn.sigmoid(gate_value)
    return gate_value * gate_sig, gate_sig


def turn_kernel(scalars, *refs):
    groups, out = refs[:6], refs[6]
    slot = 0
    for group in groups:
        count, tokens, _ = group.shape
        for i in range(count):
            slot += 1
            at = pl.multiple_of(scalars[slot] * tokens, tokens)
            out[:, pl.ds(at, tokens)] = group[i].T


def turned(scalars, groups, depth):
    tokens = groups[0].shape[1]
    total = 16 * tokens
    tile = min(256, depth)
    tiles = depth // tile
    return pl.pallas_call(
        turn_kernel,
        grid_spec=pltpu.PrefetchScalarGridSpec(
            num_scalar_prefetch=1,
            grid=(tiles,),
            in_specs=[
                pl.BlockSpec((g.shape[0], tokens, tile), lambda j, s: (0, 0, s[0] * tiles + j))
                for g in groups
            ],
            out_specs=pl.BlockSpec((tile, total), lambda j, s: (j, 0)),
        ),
        out_shape=jax.ShapeDtypeStruct((depth, total), BF16),
        compiler_params=pltpu.CompilerParams(vmem_limit_bytes=60 * 2**20),
        cost_estimate=pl.CostEstimate(
            flops=0, bytes_accessed=4 * total * depth, transcendentals=0
        ),
    )(scalars, *groups)


def product_kernel(scale, features, hidden, *refs):
    out = refs[-1]
    part = jnp.dot(features[...], hidden[...], preferred_element_type=F32)
    out[...] = (part * scale).astype(BF16)


def down_product(features, hidden, scale, first, last, before=None):
    depth, total = features.shape
    units = hidden.shape[1]
    tile = min(256, units)
    count = units // tile
    first, last = int(count * first), int(count * last)
    return pl.pallas_call(
        functools.partial(product_kernel, scale),
        grid=(last - first,),
        in_specs=[
            pl.BlockSpec((depth, total), lambda j: (0, 0)),
            pl.BlockSpec((total, tile), lambda j: (0, first + j)),
        ]
        + ([] if before is None else [pl.BlockSpec(memory_space=pl.ANY)]),
        out_specs=pl.BlockSpec((depth, tile), lambda j: (0, first + j)),
        out_shape=jax.ShapeDtypeStruct((depth, units), BF16),
        input_output_aliases={} if before is None else {2: 0},
        compiler_params=pltpu.CompilerParams(vmem_limit_bytes=60 * 2**20),
        cost_estimate=pl.CostEstimate(
            flops=total * depth * units,
            bytes_accessed=2 * total * depth + total * units + depth * units,
            transcendentals=0,
        ),
    )(features, hidden, *([] if before is None else [before]))


def on_device(gate_pre, up_pre, grad_out, down_weight):
    row, col = lax.axis_index("row"), lax.axis_index("col")
    xh, y, core = row // (NY * NC), (row // NC) % NY, row % NC
    xl, z = col // NZ, col % NZ
    first_core = core == 0
    tokens, width = grad_out.shape
    depth, units = down_weight.shape
    half = units // 2
    cut = tokens // 2

    moves = (1, 3, 2)

    hidden = (swish(gate_pre.astype(F32))[0] * up_pre.astype(F32)).astype(BF16)
    grad_out, hidden = lax.optimization_barrier((grad_out, hidden))
    own = transpose_chips(grad_out)
    hidden_all = lax.all_gather(hidden, "row", axis=0, tiled=True)

    keep = jnp.where(first_core, down_weight[:, :half], down_weight[:, half:])
    give = jnp.where(first_core, down_weight[:, half:], down_weight[:, :half])
    own, give = lax.optimization_barrier((own, give))
    got = swap_core(give)
    weight = jnp.where(
        first_core, jnp.concatenate([keep, got], 0), jnp.concatenate([got, keep], 0)
    )

    def partial(rows):
        out = jnp.dot(rows.reshape(-1, width), weight, preferred_element_type=F32)
        return out.astype(BF16).reshape(*rows.shape[:-1], half)

    near_1, near_3, far_0 = shift_z(own, 1), shift_z(own, 3), swap_xl(own)
    near_1, near_3, far_0, weight = lax.optimization_barrier((near_1, near_3, far_0, weight))

    far_1, far_3 = shift_z(far_0, 1), shift_z(far_0, 3)
    near_mine = jnp.stack([own, near_1, near_3])
    near_other = swap_core(near_mine)
    near_up, near_down = partial(near_mine), partial(near_other)
    far_1, far_3, near_up, near_down = lax.optimization_barrier((far_1, far_3, near_up, near_down))

    ahead = shift_z(jnp.stack([near_1[:cut], far_1[:cut]]), 1)
    behind = shift_z(jnp.stack([near_3[cut:], far_3[cut:]]), 3)
    far_mine = jnp.stack([far_0, far_1, far_3])
    far_other = swap_core(far_mine)
    far_up, far_down = partial(far_mine), partial(far_other)
    ahead, behind, far_up, far_down = lax.optimization_barrier((ahead, behind, far_up, far_down))

    last_mine = jnp.concatenate([ahead, behind], 1)
    last_other = swap_core(last_mine)
    last_up, last_down = partial(last_mine), partial(last_other)

    near_here = xl == xh
    at = [(z - y - d) % NZ for d in range(NY)]

    def side_up(is_near):
        first = jnp.where(is_near, near_up, far_up)
        return jnp.concatenate([first, jnp.where(is_near, last_up[:1], last_up[1:])], 0)

    there_up = side_up(jnp.logical_not(near_here))
    x_got = swap_xh(there_up)

    def downs(d):
        return jnp.stack(
            [block_of(group, last_down[i], at[d]) for i, group in enumerate((near_down, far_down))]
        )

    across_1, across_3 = downs(2)[:, :cut], downs(2)[:, cut:]
    across_1, across_3 = shift_y(across_1, 1), shift_y(across_3, 3)
    slots = [core]
    for i in range(6):
        owner = core if i % 2 == 0 else 1 - core
        sides = ((xl, 0), (xl, 1), (xl, 3)), ((1 - xl, 0), (1 - xl, 1), (1 - xl, 3)), ((xl, 2), (1 - xl, 2))
        slots += [(side * NY + (z - d) % NZ) * NC + owner for side, d in sides[i // 2]]
    scalars = jnp.stack(slots).astype(jnp.int32)
    groups = (near_mine, near_other, far_mine, far_other, last_mine, last_other)

    def plus(block, start, more):
        total = block[:, start : start + cut].astype(F32) + more.astype(F32)
        return lax.dynamic_update_slice(block, total.astype(BF16), (0, start, 0))

    down_1, down_3 = plus(downs(1), 0, across_1), plus(downs(3), cut, across_3)
    y_got = shift_y(down_1, 1), shift_y(down_3, 3)

    groups, near_up, far_up, last_up, near_down, far_down, last_down, _, _ = lax.optimization_barrier(
        (
            groups,
            near_up,
            far_up,
            last_up,
            near_down,
            far_down,
            last_down,
            there_up,
            (down_1, down_3),
        )
    )
    down_0 = downs(0)
    here_up = side_up(near_here)
    features = turned(scalars, groups, depth)
    scale = 1.0 / math.sqrt(hidden_all.shape[0])
    grad_down = down_product(features, hidden_all, scale, 0, PART)
    y_got, down_0, grad_down, gate_pre, up_pre = lax.optimization_barrier(
        (y_got, down_0, grad_down, gate_pre, up_pre)
    )
    near_sum, far_sum = (sum(part[i].astype(F32) for part in (down_0, *y_got)) for i in range(2))
    across = jnp.where(near_here, far_sum, near_sum).astype(BF16)
    along = jnp.where(near_here, near_sum, far_sum).astype(BF16)
    x_last, core_last = swap_xh_core(across), swap_core(along)
    x_got, here_up, _, _ = lax.optimization_barrier((x_got, here_up, across, along))

    def joined(d):
        e = jnp.where(at[d] == 2, 3, jnp.minimum(at[d], 2))
        return pick(here_up, e).astype(F32) + pick(x_got, e).astype(F32)

    last_send = {d: joined(d).astype(BF16) for d in moves}
    y_last = {d: shift_y(last_send[d], d) for d in moves}
    features, hidden_all, grad_down, _ = lax.optimization_barrier(
        (features, hidden_all, grad_down, last_send)
    )
    grad_down = down_product(features, hidden_all, scale, PART, 1, grad_down)
    y_last, x_last, core_last, grad_down = lax.optimization_barrier(
        (y_last, x_last, core_last, grad_down)
    )

    mine = joined(0) + sum(y_last[d].astype(F32) for d in moves)
    other = x_last.astype(F32) + core_last.astype(F32)
    grad_hidden = jnp.where(
        first_core, jnp.concatenate([mine, other], 1), jnp.concatenate([other, mine], 1)
    )
    gate_value, up_value = gate_pre.astype(F32), up_pre.astype(F32)
    activated, gate_sig = swish(gate_value)
    grad_gate = (grad_hidden * up_value * gate_sig * (1.0 + gate_value * (1.0 - gate_sig))).astype(
        BF16
    )
    grad_up = (grad_hidden * activated).astype(BF16)

    return (grad_gate, grad_up, grad_down)


def solution(mesh):
    in_specs = (P("row", "col"), P("row", "col"), P("row", "col"), P("row", "col"))
    out_specs = (P("row", "col"), P("row", "col"), P("row", "col"))
    return jax.shard_map(
        on_device, mesh=mesh, in_specs=in_specs, out_specs=out_specs, check_vma=False
    )
```

```python
import functools
import math

import jax
import jax.numpy as jnp
from jax import lax
from jax.experimental import pallas as pl
from jax.experimental.pallas import tpu as pltpu
from jax.sharding import PartitionSpec as P

NX, NY, NC, NL, NZ = 2, 4, 2, 2, 4
AXES = ("row", "col")
PART = 0.33
F32, BF16 = jnp.float32, jnp.bfloat16


def linear(xh, y, core, xl, z):
    return (((xh * NY + y) * NC + core) * NL + xl) * NZ + z


def send(value, target):
    pairs = []
    for xh in range(NX):
        for y in range(NY):
            for core in range(NC):
                for xl in range(NL):
                    for z in range(NZ):
                        to = target(xh, y, core, xl, z)
                        pairs.append((linear(xh, y, core, xl, z), linear(*to)))
    return lax.ppermute(value, AXES, pairs)


def swap_core(value):
    return send(value, lambda xh, y, core, xl, z: (xh, y, 1 - core, xl, z))


def swap_xh(value):
    return send(value, lambda xh, y, core, xl, z: (1 - xh, y, core, xl, z))


def swap_xh_core(value):
    return send(value, lambda xh, y, core, xl, z: (1 - xh, y, 1 - core, xl, z))


def swap_xl(value):
    return send(value, lambda xh, y, core, xl, z: (xh, y, core, 1 - xl, z))


def shift_y(value, d):
    return send(value, lambda xh, y, core, xl, z: (xh, (y + d) % NY, core, xl, z))


def shift_z(value, d):
    return send(value, lambda xh, y, core, xl, z: (xh, y, core, xl, (z + d) % NZ))


def transpose_chips(value):
    return send(value, lambda xh, y, core, xl, z: (xl, z, core, xh, y))


def pick(array, index):
    return lax.dynamic_index_in_dim(array, index, 0, keepdims=False)


def put(array, chunk, *index):
    start = (*index, *([0] * (array.ndim - len(index))))
    return lax.dynamic_update_slice(array, chunk.reshape((1,) * len(index) + chunk.shape), start)


def block_of(group, last, e):
    return jnp.where(e == 2, last, pick(group, jnp.minimum(e, 2)))


def swish(gate_value):
    gate_sig = jax.nn.sigmoid(gate_value)
    return gate_value * gate_sig, gate_sig


def turn_kernel(scalars, *refs):
    groups, out = refs[:6], refs[6]
    slot = 0
    for group in groups:
        count, tokens, _ = group.shape
        for i in range(count):
            slot += 1
            at = pl.multiple_of(scalars[slot] * tokens, tokens)
            out[:, pl.ds(at, tokens)] = group[i].T


def turned(scalars, groups, depth):
    tokens = groups[0].shape[1]
    total = 16 * tokens
    tile = min(256, depth)
    tiles = depth // tile
    return pl.pallas_call(
        turn_kernel,
        grid_spec=pltpu.PrefetchScalarGridSpec(
            num_scalar_prefetch=1,
            grid=(tiles,),
            in_specs=[
                pl.BlockSpec((g.shape[0], tokens, tile), lambda j, s: (0, 0, s[0] * tiles + j))
                for g in groups
            ],
            out_specs=pl.BlockSpec((tile, total), lambda j, s: (j, 0)),
        ),
        out_shape=jax.ShapeDtypeStruct((depth, total), BF16),
        compiler_params=pltpu.CompilerParams(vmem_limit_bytes=60 * 2**20),
        cost_estimate=pl.CostEstimate(
            flops=0, bytes_accessed=4 * total * depth, transcendentals=0
        ),
    )(scalars, *groups)


def product_kernel(scale, features, hidden, *refs):
    out = refs[-1]
    part = jnp.dot(features[...], hidden[...], preferred_element_type=F32)
    out[...] = (part * scale).astype(BF16)


def down_product(features, hidden, scale, first, last, before=None):
    depth, total = features.shape
    units = hidden.shape[1]
    tile = min(256, units)
    count = units // tile
    first, last = int(count * first), int(count * last)
    return pl.pallas_call(
        functools.partial(product_kernel, scale),
        grid=(last - first,),
        in_specs=[
            pl.BlockSpec((depth, total), lambda j: (0, 0)),
            pl.BlockSpec((total, tile), lambda j: (0, first + j)),
        ]
        + ([] if before is None else [pl.BlockSpec(memory_space=pl.ANY)]),
        out_specs=pl.BlockSpec((depth, tile), lambda j: (0, first + j)),
        out_shape=jax.ShapeDtypeStruct((depth, units), BF16),
        input_output_aliases={} if before is None else {2: 0},
        compiler_params=pltpu.CompilerParams(vmem_limit_bytes=60 * 2**20),
        cost_estimate=pl.CostEstimate(
            flops=total * depth * units,
            bytes_accessed=2 * total * depth + total * units + depth * units,
            transcendentals=0,
        ),
    )(features, hidden, *([] if before is None else [before]))


def on_device(gate_pre, up_pre, grad_out, down_weight):
    row, col = lax.axis_index("row"), lax.axis_index("col")
    xh, y, core = row // (NY * NC), (row // NC) % NY, row % NC
    xl, z = col // NZ, col % NZ
    first_core = core == 0
    tokens, width = grad_out.shape
    depth, units = down_weight.shape
    half = units // 2
    cut = tokens // 2

    moves = (1, 3, 2)

    hidden = (swish(gate_pre.astype(F32))[0] * up_pre.astype(F32)).astype(BF16)
    grad_out, hidden = lax.optimization_barrier((grad_out, hidden))
    own = transpose_chips(grad_out)
    hidden_all = lax.all_gather(hidden, "row", axis=0, tiled=True)

    keep = jnp.where(first_core, down_weight[:, :half], down_weight[:, half:])
    give = jnp.where(first_core, down_weight[:, half:], down_weight[:, :half])
    own, give = lax.optimization_barrier((own, give))
    got = swap_core(give)
    weight = jnp.where(
        first_core, jnp.concatenate([keep, got], 0), jnp.concatenate([got, keep], 0)
    )

    def partial(rows):
        out = jnp.dot(rows.reshape(-1, width), weight, preferred_element_type=F32)
        return out.astype(BF16).reshape(*rows.shape[:-1], half)

    near_1, near_3, far_0 = shift_z(own, 1), shift_z(own, 3), swap_xl(own)
    near_1, near_3, far_0, weight = lax.optimization_barrier((near_1, near_3, far_0, weight))

    far_1, far_3 = shift_z(far_0, 1), shift_z(far_0, 3)
    near_mine = jnp.stack([own, near_1, near_3])
    near_other = swap_core(near_mine)
    near_up, near_down = partial(near_mine), partial(near_other)
    far_1, far_3, near_up, near_down = lax.optimization_barrier((far_1, far_3, near_up, near_down))

    ahead = shift_z(jnp.stack([near_1[:cut], far_1[:cut]]), 1)
    behind = shift_z(jnp.stack([near_3[cut:], far_3[cut:]]), 3)
    far_mine = jnp.stack([far_0, far_1, far_3])
    far_other = swap_core(far_mine)
    far_up, far_down = partial(far_mine), partial(far_other)
    ahead, behind, far_up, far_down = lax.optimization_barrier((ahead, behind, far_up, far_down))

    last_mine = jnp.concatenate([ahead, behind], 1)
    last_other = swap_core(last_mine)
    last_up, last_down = partial(last_mine), partial(last_other)

    near_here = xl == xh
    at = [(z - y - d) % NZ for d in range(NY)]

    def side_up(is_near):
        first = jnp.where(is_near, near_up, far_up)
        return jnp.concatenate([first, jnp.where(is_near, last_up[:1], last_up[1:])], 0)

    there_up = side_up(jnp.logical_not(near_here))
    x_got = swap_xh(there_up)

    def downs(d):
        return jnp.stack(
            [block_of(group, last_down[i], at[d]) for i, group in enumerate((near_down, far_down))]
        )

    across_1, across_3 = downs(2)[:, :cut], downs(2)[:, cut:]
    across_1, across_3 = shift_y(across_1, 1), shift_y(across_3, 3)
    slots = [core]
    for i in range(6):
        owner = core if i % 2 == 0 else 1 - core
        sides = ((xl, 0), (xl, 1), (xl, 3)), ((1 - xl, 0), (1 - xl, 1), (1 - xl, 3)), ((xl, 2), (1 - xl, 2))
        slots += [(side * NY + (z - d) % NZ) * NC + owner for side, d in sides[i // 2]]
    scalars = jnp.stack(slots).astype(jnp.int32)
    groups = (near_mine, near_other, far_mine, far_other, last_mine, last_other)

    def plus(block, start, more):
        total = block[:, start : start + cut].astype(F32) + more.astype(F32)
        return lax.dynamic_update_slice(block, total.astype(BF16), (0, start, 0))

    down_1, down_3 = plus(downs(1), 0, across_1), plus(downs(3), cut, across_3)
    y_got = shift_y(down_1, 1), shift_y(down_3, 3)

    groups, near_up, far_up, last_up, near_down, far_down, last_down, _, _ = lax.optimization_barrier(
        (
            groups,
            near_up,
            far_up,
            last_up,
            near_down,
            far_down,
            last_down,
            there_up,
            (down_1, down_3),
        )
    )
    down_0 = downs(0)
    here_up = side_up(near_here)
    features = turned(scalars, groups, depth)
    scale = 1.0 / math.sqrt(hidden_all.shape[0])
    grad_down = down_product(features, hidden_all, scale, 0, PART)
    x_got, here_up, grad_down, gate_pre, up_pre = lax.optimization_barrier(
        (x_got, here_up, grad_down, gate_pre, up_pre)
    )

    def joined(d):
        e = jnp.where(at[d] == 2, 3, jnp.minimum(at[d], 2))
        return pick(here_up, e).astype(F32) + pick(x_got, e).astype(F32)

    last_send = {d: joined(d).astype(BF16) for d in moves}
    y_last = {d: shift_y(last_send[d], d) for d in moves}
    y_got, down_0, _ = lax.optimization_barrier((y_got, down_0, last_send))
    near_sum, far_sum = (sum(part[i].astype(F32) for part in (down_0, *y_got)) for i in range(2))
    across = jnp.where(near_here, far_sum, near_sum).astype(BF16)
    along = jnp.where(near_here, near_sum, far_sum).astype(BF16)
    x_last, core_last = swap_xh_core(across), swap_core(along)
    features, hidden_all, grad_down, _, _ = lax.optimization_barrier(
        (features, hidden_all, grad_down, across, along)
    )
    grad_down = down_product(features, hidden_all, scale, PART, 1, grad_down)
    y_last, x_last, core_last, grad_down = lax.optimization_barrier(
        (y_last, x_last, core_last, grad_down)
    )

    mine = joined(0) + sum(y_last[d].astype(F32) for d in moves)
    other = x_last.astype(F32) + core_last.astype(F32)
    grad_hidden = jnp.where(
        first_core, jnp.concatenate([mine, other], 1), jnp.concatenate([other, mine], 1)
    )
    gate_value, up_value = gate_pre.astype(F32), up_pre.astype(F32)
    activated, gate_sig = swish(gate_value)
    grad_gate = (grad_hidden * up_value * gate_sig * (1.0 + gate_value * (1.0 - gate_sig))).astype(
        BF16
    )
    grad_up = (grad_hidden * activated).astype(BF16)

    return (grad_gate, grad_up, grad_down)


def solution(mesh):
    in_specs = (P("row", "col"), P("row", "col"), P("row", "col"), P("row", "col"))
    out_specs = (P("row", "col"), P("row", "col"), P("row", "col"))
    return jax.shard_map(
        on_device, mesh=mesh, in_specs=in_specs, out_specs=out_specs, check_vma=False
    )
```

```python
import functools
import math

import jax
import jax.numpy as jnp
from jax import lax
from jax.experimental import pallas as pl
from jax.experimental.pallas import tpu as pltpu
from jax.sharding import PartitionSpec as P

NX, NY, NC, NL, NZ = 2, 4, 2, 2, 4
AXES = ("row", "col")
PART = 0.33
F32, BF16 = jnp.float32, jnp.bfloat16


def linear(xh, y, core, xl, z):
    return (((xh * NY + y) * NC + core) * NL + xl) * NZ + z


def send(value, target):
    pairs = []
    for xh in range(NX):
        for y in range(NY):
            for core in range(NC):
                for xl in range(NL):
                    for z in range(NZ):
                        to = target(xh, y, core, xl, z)
                        pairs.append((linear(xh, y, core, xl, z), linear(*to)))
    return lax.ppermute(value, AXES, pairs)


def swap_core(value):
    return send(value, lambda xh, y, core, xl, z: (xh, y, 1 - core, xl, z))


def swap_xh(value):
    return send(value, lambda xh, y, core, xl, z: (1 - xh, y, core, xl, z))


def swap_xh_core(value):
    return send(value, lambda xh, y, core, xl, z: (1 - xh, y, 1 - core, xl, z))


def swap_xl(value):
    return send(value, lambda xh, y, core, xl, z: (xh, y, core, 1 - xl, z))


def shift_y(value, d):
    return send(value, lambda xh, y, core, xl, z: (xh, (y + d) % NY, core, xl, z))


def shift_z(value, d):
    return send(value, lambda xh, y, core, xl, z: (xh, y, core, xl, (z + d) % NZ))


def transpose_chips(value):
    return send(value, lambda xh, y, core, xl, z: (xl, z, core, xh, y))


def pick(array, index):
    return lax.dynamic_index_in_dim(array, index, 0, keepdims=False)


def put(array, chunk, *index):
    start = (*index, *([0] * (array.ndim - len(index))))
    return lax.dynamic_update_slice(array, chunk.reshape((1,) * len(index) + chunk.shape), start)


def block_of(group, last, e):
    return jnp.where(e == 2, last, pick(group, jnp.minimum(e, 2)))


def swish(gate_value):
    gate_sig = jax.nn.sigmoid(gate_value)
    return gate_value * gate_sig, gate_sig


def turn_kernel(scalars, *refs):
    groups, out = refs[:6], refs[6]
    slot = 0
    for group in groups:
        count, tokens, _ = group.shape
        for i in range(count):
            slot += 1
            at = pl.multiple_of(scalars[slot] * tokens, tokens)
            out[:, pl.ds(at, tokens)] = group[i].T


def turned(scalars, groups, depth):
    tokens = groups[0].shape[1]
    total = 16 * tokens
    tile = min(256, depth)
    tiles = depth // tile
    return pl.pallas_call(
        turn_kernel,
        grid_spec=pltpu.PrefetchScalarGridSpec(
            num_scalar_prefetch=1,
            grid=(tiles,),
            in_specs=[
                pl.BlockSpec((g.shape[0], tokens, tile), lambda j, s: (0, 0, s[0] * tiles + j))
                for g in groups
            ],
            out_specs=pl.BlockSpec((tile, total), lambda j, s: (j, 0)),
        ),
        out_shape=jax.ShapeDtypeStruct((depth, total), BF16),
        compiler_params=pltpu.CompilerParams(vmem_limit_bytes=60 * 2**20),
        cost_estimate=pl.CostEstimate(
            flops=0, bytes_accessed=4 * total * depth, transcendentals=0
        ),
    )(scalars, *groups)


def product_kernel(scale, features, hidden, *refs):
    out = refs[-1]
    part = jnp.dot(features[...], hidden[...], preferred_element_type=F32)
    out[...] = (part * scale).astype(BF16)


def down_product(features, hidden, scale, first, last, before=None):
    depth, total = features.shape
    units = hidden.shape[1]
    tile = min(256, units)
    count = units // tile
    first, last = int(count * first), int(count * last)
    return pl.pallas_call(
        functools.partial(product_kernel, scale),
        grid=(last - first,),
        in_specs=[
            pl.BlockSpec((depth, total), lambda j: (0, 0)),
            pl.BlockSpec((total, tile), lambda j: (0, first + j)),
        ]
        + ([] if before is None else [pl.BlockSpec(memory_space=pl.ANY)]),
        out_specs=pl.BlockSpec((depth, tile), lambda j: (0, first + j)),
        out_shape=jax.ShapeDtypeStruct((depth, units), BF16),
        input_output_aliases={} if before is None else {2: 0},
        compiler_params=pltpu.CompilerParams(vmem_limit_bytes=60 * 2**20),
        cost_estimate=pl.CostEstimate(
            flops=total * depth * units,
            bytes_accessed=2 * total * depth + total * units + depth * units,
            transcendentals=0,
        ),
    )(features, hidden, *([] if before is None else [before]))


def on_device(gate_pre, up_pre, grad_out, down_weight):
    row, col = lax.axis_index("row"), lax.axis_index("col")
    xh, y, core = row // (NY * NC), (row // NC) % NY, row % NC
    xl, z = col // NZ, col % NZ
    first_core = core == 0
    tokens, width = grad_out.shape
    depth, units = down_weight.shape
    half = units // 2
    cut = tokens // 2

    moves = (1, 3, 2)

    hidden = (swish(gate_pre.astype(F32))[0] * up_pre.astype(F32)).astype(BF16)
    grad_out, hidden = lax.optimization_barrier((grad_out, hidden))
    own = transpose_chips(grad_out)
    hidden_all = lax.all_gather(hidden, "row", axis=0, tiled=True)

    keep = jnp.where(first_core, down_weight[:, :half], down_weight[:, half:])
    give = jnp.where(first_core, down_weight[:, half:], down_weight[:, :half])
    own, give = lax.optimization_barrier((own, give))
    got = swap_core(give)
    weight = jnp.where(
        first_core, jnp.concatenate([keep, got], 0), jnp.concatenate([got, keep], 0)
    )

    def partial(rows):
        out = jnp.dot(rows.reshape(-1, width), weight, preferred_element_type=F32)
        return out.astype(BF16).reshape(*rows.shape[:-1], half)

    near_1, near_3, far_0 = shift_z(own, 1), shift_z(own, 3), swap_xl(own)
    near_1, near_3, far_0, weight = lax.optimization_barrier((near_1, near_3, far_0, weight))

    far_1, far_3 = shift_z(far_0, 1), shift_z(far_0, 3)
    near_mine = jnp.stack([own, near_1, near_3])
    near_other = swap_core(near_mine)
    near_up, near_down = partial(near_mine), partial(near_other)
    far_1, far_3, near_up, near_down = lax.optimization_barrier((far_1, far_3, near_up, near_down))

    ahead = shift_z(jnp.stack([near_1[:cut], far_1[:cut]]), 1)
    behind = shift_z(jnp.stack([near_3[cut:], far_3[cut:]]), 3)
    far_mine = jnp.stack([far_0, far_1, far_3])
    far_other = swap_core(far_mine)
    far_up, far_down = partial(far_mine), partial(far_other)
    ahead, behind, far_up, far_down = lax.optimization_barrier((ahead, behind, far_up, far_down))

    last_mine = jnp.concatenate([ahead, behind], 1)
    last_other = swap_core(last_mine)
    last_up, last_down = partial(last_mine), partial(last_other)

    near_here = xl == xh
    at = [(z - y - d) % NZ for d in range(NY)]

    def side_up(is_near):
        first = jnp.where(is_near, near_up, far_up)
        return jnp.concatenate([first, jnp.where(is_near, last_up[:1], last_up[1:])], 0)

    there_up = side_up(jnp.logical_not(near_here))
    x_got = swap_xh(there_up)

    def downs(d):
        return jnp.stack(
            [block_of(group, last_down[i], at[d]) for i, group in enumerate((near_down, far_down))]
        )

    across_1, across_3 = downs(2)[:, :cut], downs(2)[:, cut:]
    across_1, across_3 = shift_y(across_1, 1), shift_y(across_3, 3)
    slots = [core]
    for i in range(6):
        owner = core if i % 2 == 0 else 1 - core
        sides = ((xl, 0), (xl, 1), (xl, 3)), ((1 - xl, 0), (1 - xl, 1), (1 - xl, 3)), ((xl, 2), (1 - xl, 2))
        slots += [(side * NY + (z - d) % NZ) * NC + owner for side, d in sides[i // 2]]
    scalars = jnp.stack(slots).astype(jnp.int32)
    groups = (near_mine, near_other, far_mine, far_other, last_mine, last_other)

    here_up, down_0 = side_up(near_here), downs(0)
    across_1, across_3, here_up, down_0 = lax.optimization_barrier(
        (across_1, across_3, here_up, down_0)
    )

    def plus(block, start, more):
        total = block[:, start : start + cut].astype(F32) + more.astype(F32)
        return lax.dynamic_update_slice(block, total.astype(BF16), (0, start, 0))

    down_1, down_3 = plus(downs(1), 0, across_1), plus(downs(3), cut, across_3)
    y_got = shift_y(down_1, 1), shift_y(down_3, 3)

    groups, near_up, far_up, last_up, near_down, far_down, last_down, _, _ = lax.optimization_barrier(
        (
            groups,
            near_up,
            far_up,
            last_up,
            near_down,
            far_down,
            last_down,
            there_up,
            (down_1, down_3),
        )
    )
    features = turned(scalars, groups, depth)
    scale = 1.0 / math.sqrt(hidden_all.shape[0])
    grad_down = down_product(features, hidden_all, scale, 0, PART)
    x_got, here_up, grad_down, gate_pre, up_pre = lax.optimization_barrier(
        (x_got, here_up, grad_down, gate_pre, up_pre)
    )

    def joined(d):
        e = jnp.where(at[d] == 2, 3, jnp.minimum(at[d], 2))
        return pick(here_up, e).astype(F32) + pick(x_got, e).astype(F32)

    last_send = {d: joined(d).astype(BF16) for d in moves}
    y_last = {d: shift_y(last_send[d], d) for d in moves}
    y_got, down_0, _ = lax.optimization_barrier((y_got, down_0, last_send))
    near_sum, far_sum = (sum(part[i].astype(F32) for part in (down_0, *y_got)) for i in range(2))
    across = jnp.where(near_here, far_sum, near_sum).astype(BF16)
    along = jnp.where(near_here, near_sum, far_sum).astype(BF16)
    x_last, core_last = swap_xh_core(across), swap_core(along)
    features, hidden_all, grad_down, _, _ = lax.optimization_barrier(
        (features, hidden_all, grad_down, across, along)
    )
    grad_down = down_product(features, hidden_all, scale, PART, 1, grad_down)
    y_last, x_last, core_last, grad_down = lax.optimization_barrier(
        (y_last, x_last, core_last, grad_down)
    )

    mine = joined(0) + sum(y_last[d].astype(F32) for d in moves)
    other = x_last.astype(F32) + core_last.astype(F32)
    grad_hidden = jnp.where(
        first_core, jnp.concatenate([mine, other], 1), jnp.concatenate([other, mine], 1)
    )
    gate_value, up_value = gate_pre.astype(F32), up_pre.astype(F32)
    activated, gate_sig = swish(gate_value)
    grad_gate = (grad_hidden * up_value * gate_sig * (1.0 + gate_value * (1.0 - gate_sig))).astype(
        BF16
    )
    grad_up = (grad_hidden * activated).astype(BF16)

    return (grad_gate, grad_up, grad_down)


def solution(mesh):
    in_specs = (P("row", "col"), P("row", "col"), P("row", "col"), P("row", "col"))
    out_specs = (P("row", "col"), P("row", "col"), P("row", "col"))
    return jax.shard_map(
        on_device, mesh=mesh, in_specs=in_specs, out_specs=out_specs, check_vma=False
    )
```
